128 devices in a mesh: line: 16 (over x_lo, z, core), bus: 8 (over y, x_hi).
Axes of the slice: x: 4 (x_hi: 2, x_lo: 2; x = x_hi * 2 + x_lo), y: 4, z: 4, core: 2. Of those that a mesh axis runs over, the one named last changes fastest.
Arguments:
- ptdf: bfloat16 [16384, 70656], P('line', 'bus'), may hold values from -0.0234375 to 0.0234375
- injections: bfloat16 [70656, 256], P('bus', 'line'), may hold values from -6 to 6
- viol_mask: int32 [16384, 256], P('line'), may hold values 0 or 1
- viol_sign: int32 [16384], P('line'), may hold values from 0 to 1
- limit: float32 [16384], P('line'), may hold values from 0.2 to 1.5
- price: float32 [16384], P('line'), may hold values from 0.3 to 3
- owner: int32 [70656], P('bus'), may hold values from 0 to 10367, as said below
Outputs:
- gen_cut: float32 [10368, 256], P(('line', 'bus'))
The draws below stay inside these ranges and needn't reach their ends.
Inputs may be any that keep to these rules, and one draw needn't show every extreme that they name: `owner`: each bus has one owning generator; split the buses into aligned blocks of 70656 // 128 in order and the generators into groups of 10368 // 128 in order: in every block at most 5 buses belong to one group, and some group has exactly 5 in every block.
All inputs are finite; a program needn't handle non-finite values. No bound on the sum of `viol_mask` on one device may be relied on, other than what follows from the above.
Results may differ from the reference program's by a relative error of at most 0.0029.
Values may be sent and summed in bfloat16 or wider, within the bound.
No kernel may reach another device: no remote copies, remote signals or barrier semaphores. Data moves between devices by JAX's collectives and lax.ppermute only.
A program may use at most 128 MiB of HBM per device.

```python
import math
import jax
import jax.numpy as jnp
from jax import lax

LINE_DEV = 1024
BUSES = 70656
SCEN = 256
GENS = 10368
LINES = 16384
DEVICES = 128


def draw_owner(key, part):
    devices = DEVICES
    block_rows = BUSES // devices
    held_gens = GENS // devices
    first, second, third = jax.random.split(key, 3)
    order = jax.vmap(lambda k: jax.random.permutation(k, block_rows))(jax.random.split(first, devices))
    target_perm = jax.vmap(lambda k: jax.random.permutation(k, devices))(jax.random.split(second, devices))
    target = jnp.take_along_axis(target_perm, order % devices, axis=1)
    within = jax.random.randint(third, (devices, block_rows), 0, held_gens)
    return (target * held_gens + within).reshape(BUSES).astype(jnp.int32)


def set_ends(array, key, low, high):
    extent = array.shape
    spot = [jax.random.randint(jax.random.fold_in(key, axis), (), 0, extent[axis]) for axis in range(len(extent))]
    array = array.at[tuple(spot)].set(low)
    longest = extent.index(max(extent))
    spot[longest] = (spot[longest] + 1) % extent[longest]
    return array.at[tuple(spot)].set(high)


def block_levels(rng, shape, shards, least, high):
    factor_of = 1.0
    for axis_at, blocks in shards:
        steps = jax.random.uniform(jax.random.fold_in(jax.random.fold_in(rng, 6), axis_at), (blocks,), jnp.float32, least / len(shards), high / len(shards))
        factor_of = factor_of * jnp.repeat(jnp.exp(steps), shape[axis_at] // blocks).reshape((-1,) + (1,) * (len(shape) - 1 - axis_at))
    return factor_of


def normal_values(key, shape, width, bound, cuts=(), dtype=jnp.bfloat16):
    array = width * jax.random.normal(key, shape, jnp.float32)
    if cuts:
        array = array * block_levels(key, shape, cuts, -0.22, 0.18)
    return jnp.clip(array, -bound, bound).astype(dtype)


def setup_inputs(seed: int = 0) -> dict:
    streams_of = jax.random.split(jax.random.key(seed), 8)
    return {
        "ptdf": normal_values(streams_of[0], (LINES, BUSES), BUSES ** -0.5, 0.0234375, ((0, 16), (1, 8))),
        "injections": normal_values(streams_of[1], (BUSES, SCEN), 1.0, 6.0, ((0, 8), (1, 16))),
        "viol_mask": set_ends((jax.random.randint(streams_of[2], (LINES, SCEN), 0, 3) < 1).astype(jnp.int32), jax.random.fold_in(streams_of[2], 1), 0, 1),
        "viol_sign": set_ends(jax.random.randint(streams_of[3], (LINES,), 0, 2), jax.random.fold_in(streams_of[3], 1), 0, 1).astype(jnp.int32),
        "limit": jnp.clip(0.2 + 1.3 * jax.random.uniform(streams_of[4], (LINES,), jnp.float32) ** block_levels(streams_of[4], (LINES,), ((0, 16),), -0.2, 0.2), 0.2, 1.5),
        "price": jnp.clip(jnp.exp(math.log(3.0) - 2.3025851 * jax.random.uniform(streams_of[5], (LINES,), jnp.float32) ** block_levels(streams_of[5], (LINES,), ((0, 16),), -0.2, 0.2)), 0.3, 3.0),
        "owner": draw_owner(jax.random.fold_in(streams_of[7], 71), 0),
    }


def reference(ptdf, injections, viol_mask, viol_sign, limit, price, owner):
    blocks = LINES // LINE_DEV
    slab = ptdf.reshape(blocks, LINE_DEV, BUSES)
    masks = viol_mask.reshape(blocks, LINE_DEV, SCEN)
    signs = viol_sign.reshape(blocks, LINE_DEV)
    limits = limit.reshape(blocks, LINE_DEV)
    prices = price.reshape(blocks, LINE_DEV)
    inject32 = injections.astype(jnp.float32)

    def step(total, items):
        rows, mrows, srows, lrows, prows = items
        rows32 = rows.astype(jnp.float32)
        flows = jnp.dot(rows32, inject32, precision=lax.Precision.HIGHEST)
        direction = (2 * srows - 1).astype(jnp.float32)[:, None]
        dual = (mrows.astype(jnp.float32) * prows[:, None] * (direction * flows - lrows[:, None])).astype(jnp.bfloat16)
        total = total + jnp.dot(rows32.T, dual.astype(jnp.float32), precision=lax.Precision.HIGHEST)
        return total, None

    start = jnp.zeros((BUSES, SCEN), jnp.float32)
    cuts, unused = lax.scan(step, start, (slab, masks, signs, limits, prices))
    return jax.ops.segment_sum(cuts, owner, num_segments=GENS)
```

```python
import jax
import jax.numpy as jnp
from jax import lax
from jax.sharding import PartitionSpec as P

GENS = 10368
LINES_AT = 16
BUSES_AT = 8
DEVICES = LINES_AT * BUSES_AT
HELD = GENS // DEVICES
SLOTS = 8
PAIRS = [(i, i ^ 1) for i in range(LINES_AT)]
SAME_CORE = [[a + c for a in range(0, LINES_AT, 2)] for c in (0, 1)]
HALF = LINES_AT // 2


def make_dual(flows, mask_part, viol_sign, limit, price):
    direction = (2 * viol_sign - 1).astype(jnp.float32)[:, None]
    return (
        mask_part.astype(jnp.float32) * price[:, None] * (direction * flows - limit[:, None])
    ).astype(jnp.bfloat16)


def share(x, axis, ways, groups=None):
    spread = jnp.broadcast_to(x[None], (ways,) + x.shape)
    return lax.all_to_all(spread, axis, 0, 0, tiled=True, axis_index_groups=groups)


def ranks(groups):
    count = groups.shape[-1]
    same = groups[..., :, None] == groups[..., None, :]
    earlier = lax.broadcasted_iota(jnp.int32, (count, count), 0) > lax.broadcasted_iota(
        jnp.int32, (count, count), 1
    )
    return jnp.sum((same & earlier).astype(jnp.int32), axis=-1)


def local(ptdf, injections, viol_mask, viol_sign, limit, price, owner):
    line, bus = lax.axis_index("line"), lax.axis_index("bus")
    core = line % 2
    lines, buses = ptdf.shape
    rows = lines // BUSES_AT
    block = buses // LINES_AT
    scen = viol_mask.shape[1]

    owners = owner.reshape(2, HALF, block).transpose(1, 0, 2).reshape(LINES_AT, block)
    groups, within = owners // HELD, owners % HELD
    place = ranks(groups)
    mine = line * BUSES_AT + jnp.arange(BUSES_AT)
    slots = jnp.arange(SLOTS)
    hit = (groups[None, :, None, :] == mine[:, None, None, None]) & (
        place[None, :, None, :] == slots[None, None, :, None]
    )
    table = jnp.sum(jnp.where(hit, within[None, :, None, :] + 1, 0), axis=-1)
    table = lax.all_to_all(table.reshape(BUSES_AT, -1), "bus", 0, 0, tiled=True)
    table = table.reshape(BUSES_AT, LINES_AT, SLOTS).transpose(1, 0, 2).reshape(-1) - 1
    merge = (jnp.arange(HELD)[:, None] == table[None, :]).astype(jnp.float32)
    to = groups[line] * SLOTS + place[line]
    pick = (jnp.arange(DEVICES * SLOTS)[:, None] == to[None, :]).astype(jnp.float32)

    held = share(injections.T, "line", HALF, SAME_CORE).reshape(scen // 2, buses)
    other = lax.ppermute(held, "line", PAIRS)
    inject = jnp.where(
        core == 0,
        jnp.concatenate([held, other], 0),
        jnp.concatenate([other, held], 0),
    )
    partial_flows = lax.dot_general(
        ptdf, inject, (((1,), (1,)), ((), ())), preferred_element_type=jnp.float32
    )
    flows = jnp.sum(
        lax.all_to_all(partial_flows.reshape(BUSES_AT, rows, scen), "bus", 0, 0, tiled=True), 0
    )
    cut = lambda x: lax.dynamic_slice_in_dim(x, bus * rows, rows, 0)
    width = scen // LINES_AT
    mask = cut(viol_mask).reshape(rows, HALF, 2, width).transpose(0, 2, 1, 3).reshape(rows, scen)
    dual = make_dual(flows, mask, cut(viol_sign), cut(limit), cut(price))
    dual = share(dual, "bus", BUSES_AT).reshape(lines, scen)

    cuts = lax.dot_general(
        ptdf, dual, (((0,), (0,)), ((), ())), preferred_element_type=jnp.float32
    )
    keep = lax.dynamic_slice_in_dim(cuts, core * (buses // 2), buses // 2, 0)
    give = lax.dynamic_slice_in_dim(cuts, (1 - core) * (buses // 2), buses // 2, 0)
    got = lax.ppermute(give.astype(jnp.bfloat16), "line", PAIRS)
    chip = (keep + got.astype(jnp.float32)).astype(jnp.bfloat16)
    parts = lax.all_to_all(
        chip.reshape(HALF, block, scen), "line", 0, 0, tiled=True, axis_index_groups=SAME_CORE
    )
    summed = jnp.sum(parts.astype(jnp.float32), 0)

    send = jnp.dot(pick, summed, precision=lax.Precision.HIGHEST)
    terms = lax.all_to_all(
        send.reshape(DEVICES, SLOTS, scen), ("line", "bus"), 0, 0, tiled=True
    ).reshape(DEVICES * SLOTS, scen)
    out = jnp.dot(merge, terms, precision=lax.Precision.HIGHEST)
    return out.reshape(HELD, 2, HALF, width).transpose(0, 2, 1, 3).reshape(HELD, scen)


def solution(mesh):
    placed = (
        P("line", "bus"),
        P("bus", "line"),
        P("line", None),
        P("line"),
        P("line"),
        P("line"),
        P("bus"),
    )
    return jax.shard_map(
        local, mesh=mesh, in_specs=placed, out_specs=P(("line", "bus"), None), check_vma=False
    )
```

```python
import functools

import jax
import jax.numpy as jnp
from jax import lax
from jax.experimental import pallas as pl
from jax.experimental.pallas import tpu as pltpu
from jax.sharding import PartitionSpec as P

GENS = 10368
LINES_AT = 16
BUSES_AT = 8
DEVICES = LINES_AT * BUSES_AT
HELD = GENS // DEVICES
SLOTS = 8
FILLED = 5
TILE = 128
PAIRS = [(i, i ^ 1) for i in range(LINES_AT)]
SAME_CORE = [[a + c for a in range(0, LINES_AT, 2)] for c in (0, 1)]
HALF = LINES_AT // 2
BF16, F32 = jnp.bfloat16, jnp.float32
NT = (((1,), (1,)), ((), ()))


def share(x, axis, ways, groups=None):
    spread = jnp.broadcast_to(x[None], (ways,) + x.shape)
    return lax.all_to_all(spread, axis, 0, 0, tiled=True, axis_index_groups=groups)


def ranks(groups):
    count = groups.shape[-1]
    same = groups[..., :, None] == groups[..., None, :]
    earlier = lax.broadcasted_iota(jnp.int32, (count, count), 0) > lax.broadcasted_iota(
        jnp.int32, (count, count), 1
    )
    return jnp.sum((same & earlier).astype(jnp.int32), axis=-1)


def split3(x):
    a = x.astype(BF16)
    rest = x - a.astype(F32)
    b = rest.astype(BF16)
    return a, b, (rest - b.astype(F32)).astype(BF16)


def call(kernel, out, cost, operands, scalars=(), slab=None, scratch=(), out_specs=None):
    whole = pl.BlockSpec(memory_space=pltpu.VMEM)
    specs = [whole] * len(operands)
    if slab:
        specs[0] = pl.BlockSpec(memory_space=pl.ANY)
        shape, parts = slab
        scratch = [pltpu.VMEM(shape, BF16), pltpu.SemaphoreType.DMA((parts,)), *scratch]
    return pl.pallas_call(
        kernel,
        out_shape=out,
        in_specs=[pl.BlockSpec(memory_space=pltpu.SMEM)] * len(scalars) + specs,
        out_specs=out_specs or whole,
        scratch_shapes=scratch,
        compiler_params=pltpu.CompilerParams(vmem_limit_bytes=40 << 20),
        cost_estimate=pl.CostEstimate(flops=cost[0], bytes_accessed=cost[1], transcendentals=0),
    )(*scalars, *operands)


def flows_kernel(ptdf, held, other, out, slab, sems):
    step = ptdf.shape[0] // sems.shape[0]
    copies = [
        pltpu.make_async_copy(ptdf.at[at], slab.at[at], sems.at[i])
        for i, at in enumerate(pl.ds(i * step, step) for i in range(sems.shape[0]))
    ]
    for copy in copies:
        copy.start()
    right = jnp.concatenate([held[...], other[...]], 0)
    for i, copy in enumerate(copies):
        copy.wait()
        at = slice(i * step, (i + 1) * step)
        out[at, :] = lax.dot_general(slab[at, :], right, NT, preferred_element_type=F32)


def dual_kernel(core, parts, mask, sign, limit, price, out):
    flows = parts[0]
    for i in range(1, parts.shape[0]):
        flows = flows + parts[i]
    flows = flows.T
    half = flows.shape[0] // 2
    swapped = jnp.concatenate([flows[half:], flows[:half]], 0)
    flows = jnp.where(core[0] == 0, flows, swapped)
    direction = (2 * sign[...] - 1).astype(F32)
    dual = (mask[...].astype(F32) * price[...] * (direction * flows - limit[...])).astype(BF16)
    for i in range(out.shape[0]):
        out[i] = dual


def cut_rows(start, ptdf, dual, slab, sems, put):
    step = slab.shape[1] // sems.shape[0]
    copies = [
        pltpu.make_async_copy(
            ptdf.at[:, pl.ds(pl.multiple_of(start + i * step, TILE), step)],
            slab.at[:, pl.ds(i * step, step)],
            sems.at[i],
        )
        for i in range(sems.shape[0])
    ]
    for copy in copies:
        copy.start()
    left = jnp.concatenate([dual[b] for b in range(dual.shape[0])], 1)
    for i, copy in enumerate(copies):
        copy.wait()
        tile = slab[:, i * step : (i + 1) * step]
        put(slice(i * step, (i + 1) * step), jnp.dot(left, tile, preferred_element_type=F32).T)


def give_kernel(core, ptdf, dual, out, slab, sems, *, first):
    def put(at, rows):
        out[at, :] = rows.astype(BF16)

    cut_rows((1 - core[0]) * first, ptdf, dual, slab, sems, put)


def keep_kernel(core, ptdf, dual, got, out, slab, sems, held, sem, *, first):
    def put(at, rows):
        held[at, :] = (rows + got[at, :].astype(F32)).astype(BF16)

    cut_rows(core[0] * first, ptdf, dual, slab, sems, put)
    spare = held.shape[0] - out.shape[0]
    copy = pltpu.make_async_copy(
        held.at[pl.ds(pl.multiple_of(core[0] * spare, 16), out.shape[0])], out, sem
    )
    copy.start()
    copy.wait()


def pick_kernel(to, what, parts, out):
    total = parts[0].astype(F32)
    for i in range(1, parts.shape[0]):
        total = total + parts[i].astype(F32)
    at = lax.broadcasted_iota(jnp.int32, (out.shape[0], to.shape[1]), 0)
    pick = (at == to[0:1, :]).astype(BF16)
    mark = (at == to[1:2, :]).astype(BF16)
    slot = lax.broadcasted_iota(jnp.int32, (to.shape[1], out.shape[1]), 1)
    names = jnp.where(slot == what[:, 0:1], what[:, 1:2], 0).astype(F32).astype(BF16)
    dot = lambda x, y: jnp.dot(x, y, preferred_element_type=F32)
    a, b, c = split3(total)
    out[...] = dot(pick, a) + dot(pick, b) + dot(pick, c) + dot(mark, names)


def merge_kernel(terms, out):
    rows, scen = out.shape
    dot = lambda x, y: jnp.dot(x, y, preferred_element_type=F32)
    names = terms[:, SLOTS - 1, :].T
    gen = lax.broadcasted_iota(jnp.int32, (rows, DEVICES), 0).astype(F32) + 1
    total = jnp.zeros((rows, scen), F32)
    for i in range(FILLED):
        merge = (gen == names[i : i + 1, :]).astype(BF16)
        a, b, c = split3(terms[:, i, :])
        total = total + dot(merge, a) + dot(merge, b) + dot(merge, c)
    width = scen // LINES_AT
    at = lax.broadcasted_iota(jnp.int32, (scen, scen), 0)
    goes = at - at
    for i in range(LINES_AT):
        goes = jnp.where(at // width == i, at + ((i % HALF) * 2 + i // HALF - i) * width, goes)
    order = (goes == lax.broadcasted_iota(jnp.int32, (scen, scen), 1)).astype(BF16)
    a, b, c = split3(total)
    out[...] = dot(a, order) + dot(b, order) + dot(c, order)


def local(ptdf, injections, viol_mask, viol_sign, limit, price, owner):
    line, bus = lax.axis_index("line"), lax.axis_index("bus")
    core = line % 2
    at_core = core.astype(jnp.int32)[None]
    lines, buses = ptdf.shape
    rows = lines // BUSES_AT
    block = buses // LINES_AT
    half = buses // 2
    first = half // TILE * TILE
    window = buses - first
    scen = viol_mask.shape[1]
    width = scen // LINES_AT
    shape = jax.ShapeDtypeStruct
    held = share(injections.T, "line", HALF, SAME_CORE).reshape(scen // 2, buses)

    owners = lax.dynamic_slice_in_dim(owner, (core * HALF + line // 2) * block, block, 0)
    groups, within = owners // HELD, owners % HELD
    place = ranks(groups)
    to = jnp.stack([groups * SLOTS + place, groups * SLOTS + SLOTS - 1])
    what = jnp.stack([place, within + 1], axis=1)
    cut = lambda x: lax.dynamic_slice_in_dim(x, bus * rows, rows, 0)
    mask = cut(viol_mask).T.reshape(HALF, 2, width, rows).transpose(1, 0, 2, 3).reshape(scen, rows)
    sign, limit, price = (cut(x)[None, :] for x in (viol_sign, limit, price))
    held, to, what, mask, sign, limit, price = lax.optimization_barrier(
        (held, to, what, mask, sign, limit, price)
    )

    other = lax.ppermute(held, "line", PAIRS)
    work = 2 * lines * buses * scen
    partial_flows = call(
        flows_kernel,
        shape((lines, scen), F32),
        (work, 2 * lines * buses),
        (ptdf, held, other),
        slab=((lines, buses), 4),
    )
    parts = lax.all_to_all(partial_flows.reshape(BUSES_AT, rows, scen), "bus", 0, 0, tiled=True)
    dual = call(
        dual_kernel,
        shape((BUSES_AT, scen, rows), BF16),
        (10 * rows * scen, 8 * lines * scen),
        (parts, mask, sign, limit, price),
        (at_core,),
    )
    dual = lax.all_to_all(dual, "bus", 0, 0, tiled=True)

    give = call(
        functools.partial(give_kernel, first=first),
        shape((window, scen), BF16),
        (work // 2, lines * buses),
        (ptdf, dual),
        (at_core,),
        slab=((lines, window), 5),
    )
    got = lax.ppermute(give, "line", PAIRS)
    chip = call(
        functools.partial(keep_kernel, first=first),
        shape((half, scen), BF16),
        (work // 2, lines * buses),
        (ptdf, dual, got),
        (at_core,),
        slab=((lines, window), 5),
        scratch=[pltpu.VMEM((window, scen), BF16), pltpu.SemaphoreType.DMA],
        out_specs=pl.BlockSpec(memory_space=pl.ANY),
    )
    parts = lax.all_to_all(
        chip.reshape(HALF, block, scen), "line", 0, 0, tiled=True, axis_index_groups=SAME_CORE
    )
    send = call(
        pick_kernel,
        shape((DEVICES * SLOTS, scen), F32),
        (6 * DEVICES * SLOTS * block * scen, 2 * half * scen),
        (to, what, parts),
    )
    terms = lax.all_to_all(
        send.reshape(DEVICES, SLOTS, scen), ("line", "bus"), 0, 0, tiled=True
    )
    return call(
        merge_kernel,
        shape((HELD, scen), F32),
        (6 * DEVICES * SLOTS * HELD * scen, 4 * DEVICES * SLOTS * scen),
        (terms,),
    )


def solution(mesh):
    placed = (
        P("line", "bus"),
        P("bus", "line"),
        P("line", None),
        P("line"),
        P("line"),
        P("line"),
        P("bus"),
    )
    return jax.shard_map(
        local, mesh=mesh, in_specs=placed, out_specs=P(("line", "bus"), None), check_vma=False
    )
```

```python
import jax
import jax.numpy as jnp
import numpy as np
from jax import lax
from jax.experimental import pallas as pl
from jax.experimental.pallas import tpu as pltpu
from jax.sharding import PartitionSpec as P

GENS = 10368
LINES_AT = 16
BUSES_AT = 8
DEVICES = LINES_AT * BUSES_AT
HELD = GENS // DEVICES
SLOTS = 8
TILE = 128
PAIRS = [(i, i ^ 1) for i in range(LINES_AT)]
SAME_CORE = [[a + c for a in range(0, LINES_AT, 2)] for c in (0, 1)]
HALF = LINES_AT // 2
BF16, F32 = jnp.bfloat16, jnp.float32
NT = (((1,), (1,)), ((), ()))


def along(dx, dz, dcore):
    pairs = []
    for x in range(2):
        for z in range(4):
            for core in range(2):
                to = ((x + dx) % 2, (z + dz) % 4, (core + dcore) % 2)
                pairs.append((x * 8 + z * 2 + core, to[0] * 8 + to[1] * 2 + to[2]))
    return pairs


ORDER = [
    [(0, 0, 0), (0, 0, 1), (1, 0, 0), (1, 0, 1), (0, 3, 1), (0, 1, 1)],
    [(0, 3, 0), (1, 3, 0), (0, 1, 0), (1, 1, 0), (1, 3, 1), (1, 1, 1)],
    [(0, 2, 1), (1, 2, 1), (0, 2, 0), (1, 2, 0)],
]


def gather(block, ready):
    move = lambda x, *to: lax.ppermute(x, "line", along(*to))
    stack = lambda *x: jnp.concatenate(x, 0)
    half = block.shape[0] // 2
    low, high = block[:half], block[half:]
    high_1, high_3 = move(high, 0, 1, 0), move(high, 0, 3, 0)
    beside = move(block, 1, 0, 0)
    high_2 = move(high_1, 0, 1, 0)
    pair = stack(low, beside[:half])
    pair_1, pair_3 = move(pair, 0, 1, 0), move(pair, 0, 3, 0)
    high_z = stack(high_1, high_3)
    high_zx = move(high_z, 1, 0, 0)
    high_2x = move(high_2, 1, 0, 0)
    pair_1, pair_3, ready = lax.optimization_barrier((pair_1, pair_3, ready))
    low_2, beside_2 = move(pair_1[:half], 0, 1, 0), move(pair_3[half:], 0, 3, 0)
    pieces = [
        stack(block, beside, high_z),
        stack(pair_1, pair_3, high_zx),
        stack(high_2, high_2x, low_2, beside_2),
    ]
    return pieces + [move(piece, 0, 0, 1) for piece in pieces], ready


def gathered(line, width):
    spots = np.array([(*at, core) for core in (0, 1) for at in sum(ORDER, [])])
    dx, dz, half, core = (np.repeat(spots[:, i], width // 2) for i in range(4))
    at = np.arange(dx.shape[0]) % (width // 2) + half * (width // 2)
    x, z, mine = line // 8, line // 2 % 4, line % 2
    device = (x + dx) % 2 * 8 + (z + dz) % 4 * 2 + (mine + core) % 2
    return device * width + at


def ranks(groups):
    count = groups.shape[-1]
    same = groups[..., :, None] == groups[..., None, :]
    earlier = lax.broadcasted_iota(jnp.int32, (count, count), 0) > lax.broadcasted_iota(
        jnp.int32, (count, count), 1
    )
    return jnp.sum((same & earlier).astype(jnp.int32), axis=-1)


def split3(x):
    a = x.astype(BF16)
    rest = x - a.astype(F32)
    b = rest.astype(BF16)
    return a, b, (rest - b.astype(F32)).astype(BF16)


def call(kernel, out, cost, operands, scalars=(), slab=None, limit=24):
    whole = pl.BlockSpec(memory_space=pltpu.VMEM)
    specs, scratch = [whole] * len(operands), []
    if slab:
        specs[0] = pl.BlockSpec(memory_space=pl.ANY)
        shape, parts = slab
        scratch = [pltpu.VMEM(shape, BF16), pltpu.SemaphoreType.DMA((parts,))]
    return pl.pallas_call(
        kernel,
        out_shape=out,
        in_specs=[pl.BlockSpec(memory_space=pltpu.SMEM)] * len(scalars) + specs,
        out_specs=whole,
        scratch_shapes=scratch,
        compiler_params=pltpu.CompilerParams(vmem_limit_bytes=limit << 20),
        cost_estimate=pl.CostEstimate(flops=cost[0], bytes_accessed=cost[1], transcendentals=0),
    )(*scalars, *operands)


def in_turn(copies, work):
    for copy in copies[:2]:
        copy.start()
    for i, copy in enumerate(copies):
        copy.wait()
        if i + 2 < len(copies):
            copies[i + 2].start()
        work(i)


def flows_kernel(ptdf, *refs):
    *pieces, out = refs
    right = jnp.concatenate([piece[...] for piece in pieces], 0)
    out[...] = lax.dot_general(ptdf[...], right, NT, preferred_element_type=F32)


def dual_kernel(goes, parts, mask, sign, limit, price, out):
    flows = jnp.sum(parts[...], 0)
    scen = flows.shape[1]
    order = (lax.broadcasted_iota(jnp.int32, (scen, scen), 0) == goes[...]).astype(BF16)
    dot = lambda x: lax.dot_general(order, x, NT, preferred_element_type=F32)
    a, b, c = split3(flows)
    flows = dot(a) + dot(b) + dot(c)
    direction = (2 * sign[...] - 1).astype(F32)
    dual = (mask[...].astype(F32) * price[...] * (direction * flows - limit[...])).astype(BF16)
    for i in range(out.shape[0]):
        out[i] = dual


def cut_rows(start, ptdf, dual, slab, sems, put):
    step = slab.shape[1] // sems.shape[0]
    left = jnp.concatenate([dual[b] for b in range(dual.shape[0])], 1)

    def work(i):
        at = slice(i * step, (i + 1) * step)
        put(at, jnp.dot(left, slab[:, at], preferred_element_type=F32).T)

    in_turn(
        [
            pltpu.make_async_copy(
                ptdf.at[:, pl.ds(pl.multiple_of(start + i * step, TILE), step)],
                slab.at[:, pl.ds(i * step, step)],
                sems.at[i],
            )
            for i in range(sems.shape[0])
        ],
        work,
    )


def cuts_kernel(start, ptdf, dual, out, slab, sems):
    def put(at, rows):
        out[at, :] = rows.astype(out.dtype)

    cut_rows(start[0], ptdf, dual, slab, sems, put)


def add_kernel(spare, keep, got, out):
    at = pl.ds(pl.multiple_of(spare[0], 16), out.shape[0])
    out[...] = (keep[at, :] + got[at, :].astype(F32)).astype(BF16)


def pick_kernel(plan, parts, out):
    total = jnp.sum(parts[...].astype(F32), 0)
    at = lax.broadcasted_iota(jnp.int32, (out.shape[0], plan.shape[1]), 0)
    pick = (at == plan[0:1, :]).astype(BF16)
    mark = (at == plan[1:2, :]).astype(BF16)
    slot = lax.broadcasted_iota(jnp.int32, (out.shape[1], plan.shape[1]), 0)
    names = jnp.where(slot == plan[2:3, :], plan[3:4, :], 0).astype(F32).astype(BF16)
    dot = lambda x: jnp.dot(pick, x, preferred_element_type=F32)
    a, b, c = split3(total)
    ids = lax.dot_general(mark, names, NT, preferred_element_type=F32)
    out[...] = dot(a) + dot(b) + dot(c) + ids


def merge_kernel(terms, out):
    rows, scen = out.shape
    count = terms.shape[0] * SLOTS
    dot = lambda x, y: jnp.dot(x, y, preferred_element_type=F32)
    iota = lambda shape, axis: lax.broadcasted_iota(jnp.int32, shape, axis)
    names = terms[:, SLOTS - 1, :TILE].astype(BF16)
    spread = (iota((count // SLOTS, count), 0) == iota((count // SLOTS, count), 1) // SLOTS).astype(
        BF16
    )
    names = lax.dot_general(names, spread, (((0,), (0,)), ((), ())), preferred_element_type=F32)
    names = jnp.where(iota((SLOTS, count), 0) == iota((SLOTS, count), 1) % SLOTS, names[:SLOTS], 0.0)
    names = jnp.sum(names, 0, keepdims=True)
    merge = (iota((rows, count), 0).astype(F32) + 1 == names).astype(BF16)
    a, b, c = split3(terms[...].reshape(count, scen))
    out[...] = dot(merge, a) + dot(merge, b) + dot(merge, c)


def local(ptdf, injections, viol_mask, viol_sign, limit, price, owner):
    line, bus = lax.axis_index("line"), lax.axis_index("bus")
    core = line % 2
    lines, buses = ptdf.shape
    rows = lines // BUSES_AT
    block = buses // LINES_AT
    half = buses // 2
    first = half // TILE * TILE
    window = buses - first
    scen = viol_mask.shape[1]
    width = scen // LINES_AT
    shape = jax.ShapeDtypeStruct
    owners = lax.dynamic_slice_in_dim(owner, (core * HALF + line // 2) * block, block, 0)
    groups, within = owners // HELD, owners % HELD
    place = ranks(groups)
    plan = jnp.stack([groups * SLOTS + place, groups * SLOTS + SLOTS - 1, place, within + 1])
    cut = lambda x: lax.dynamic_slice_in_dim(x, bus * rows, rows, 0)
    mask = cut(viol_mask).T
    sign, limit, price = (cut(x)[None, :] for x in (viol_sign, limit, price))
    goes = gathered(line, width).astype(jnp.int32)[None, :]

    pieces, (plan, mask, sign, limit, price, goes) = gather(
        injections.T, (plan, mask, sign, limit, price, goes)
    )
    work = 2 * lines * buses * scen
    step = lines // 2
    partial_flows = pl.pallas_call(
        flows_kernel,
        out_shape=shape((lines, scen), F32),
        grid=(lines // step,),
        in_specs=[pl.BlockSpec((step, buses), lambda i: (i, 0))]
        + [pl.BlockSpec(memory_space=pltpu.VMEM)] * len(pieces),
        out_specs=pl.BlockSpec((step, scen), lambda i: (i, 0)),
        compiler_params=pltpu.CompilerParams(vmem_limit_bytes=32 << 20),
        cost_estimate=pl.CostEstimate(
            flops=work, bytes_accessed=2 * lines * buses, transcendentals=0
        ),
    )(ptdf, *pieces)
    parts = lax.all_to_all(partial_flows.reshape(BUSES_AT, rows, scen), "bus", 0, 0, tiled=True)
    dual = call(
        dual_kernel,
        shape((BUSES_AT, scen, rows), BF16),
        (10 * rows * scen, 8 * lines * scen),
        (goes, parts, mask, sign, limit, price),
    )
    dual = lax.all_to_all(dual, "bus", 0, 0, tiled=True)

    def cuts(start, dtype):
        return call(
            cuts_kernel,
            shape((window, scen), dtype),
            (work // 2, lines * buses),
            (pltpu.with_memory_space_constraint(ptdf, pltpu.HBM), dual),
            (start[None],),
            slab=((lines, window), 5),
        )

    core = core.astype(jnp.int32)
    got = lax.ppermute(cuts((1 - core) * first, BF16), "line", PAIRS)
    chip = call(
        add_kernel,
        shape((half, scen), BF16),
        (window * scen, 8 * window * scen),
        (cuts(core * first, F32), got),
        ((core * (window - half))[None],),
    )
    parts = lax.all_to_all(
        chip.reshape(HALF, block, scen), "line", 0, 0, tiled=True, axis_index_groups=SAME_CORE
    )
    send = call(
        pick_kernel,
        shape((DEVICES * SLOTS, scen), F32),
        (6 * DEVICES * SLOTS * block * scen, 2 * half * scen),
        (plan, parts),
    )
    terms = lax.all_to_all(
        send.reshape(DEVICES, SLOTS, scen), ("line", "bus"), 0, 0, tiled=True
    )
    return call(
        merge_kernel,
        shape((HELD, scen), F32),
        (6 * DEVICES * SLOTS * HELD * scen, 4 * DEVICES * SLOTS * scen),
        (terms,),
    )


def solution(mesh):
    placed = (
        P("line", "bus"),
        P("bus", "line"),
        P("line", None),
        P("line"),
        P("line"),
        P("line"),
        P("bus"),
    )
    return jax.shard_map(
        local, mesh=mesh, in_specs=placed, out_specs=P(("line", "bus"), None), check_vma=False
    )
```

```python
import jax
import jax.numpy as jnp
import numpy as np
from jax import lax
from jax.experimental import pallas as pl
from jax.experimental.pallas import tpu as pltpu
from jax.sharding import PartitionSpec as P

GENS = 10368
LINES_AT = 16
BUSES_AT = 8
DEVICES = LINES_AT * BUSES_AT
HELD = GENS // DEVICES
SLOTS = 8
TILE = 128
PAIRS = [(i, i ^ 1) for i in range(LINES_AT)]
HALF = LINES_AT // 2
BF16, F32 = jnp.bfloat16, jnp.float32
NT = (((1,), (1,)), ((), ()))


def along(dx, dz, dcore):
    pairs = []
    for x in range(2):
        for z in range(4):
            for core in range(2):
                to = ((x + dx) % 2, (z + dz) % 4, (core + dcore) % 2)
                pairs.append((x * 8 + z * 2 + core, to[0] * 8 + to[1] * 2 + to[2]))
    return pairs


ORDER = [
    [(0, 0, 0), (0, 0, 1), (1, 0, 0), (1, 0, 1), (0, 3, 1), (0, 1, 1)],
    [(0, 3, 0), (1, 3, 0), (0, 1, 0), (1, 1, 0), (1, 3, 1), (1, 1, 1)],
    [(0, 2, 1), (1, 2, 1), (0, 2, 0), (1, 2, 0)],
]


def gather(block, ready):
    move = lambda x, *to: lax.ppermute(x, "line", along(*to))
    stack = lambda *x: jnp.concatenate(x, 0)
    half = block.shape[0] // 2
    low, high = block[:half], block[half:]
    high_1, high_3 = move(high, 0, 1, 0), move(high, 0, 3, 0)
    beside = move(block, 1, 0, 0)
    high_2 = move(high_1, 0, 1, 0)
    pair = stack(low, beside[:half])
    pair_1, pair_3 = move(pair, 0, 1, 0), move(pair, 0, 3, 0)
    high_z = stack(high_1, high_3)
    high_zx = move(high_z, 1, 0, 0)
    high_2x = move(high_2, 1, 0, 0)
    pair_1, pair_3, ready = lax.optimization_barrier((pair_1, pair_3, ready))
    low_2, beside_2 = move(pair_1[:half], 0, 1, 0), move(pair_3[half:], 0, 3, 0)
    pieces = [
        stack(block, beside, high_z),
        stack(pair_1, pair_3, high_zx),
        stack(high_2, high_2x, low_2, beside_2),
    ]
    return pieces + [move(piece, 0, 0, 1) for piece in pieces], ready


def gathered(line, width):
    spots = np.array([(*at, core) for core in (0, 1) for at in sum(ORDER, [])])
    dx, dz, half, core = (np.repeat(spots[:, i], width // 2) for i in range(4))
    at = np.arange(dx.shape[0]) % (width // 2) + half * (width // 2)
    x, z, mine = line // 8, line // 2 % 4, line % 2
    device = (x + dx) % 2 * 8 + (z + dz) % 4 * 2 + (mine + core) % 2
    return device * width + at


def ranks(groups):
    count = groups.shape[-1]
    same = groups[..., :, None] == groups[..., None, :]
    earlier = lax.broadcasted_iota(jnp.int32, (count, count), 0) > lax.broadcasted_iota(
        jnp.int32, (count, count), 1
    )
    return jnp.sum((same & earlier).astype(jnp.int32), axis=-1)


def split3(x):
    a = x.astype(BF16)
    rest = x - a.astype(F32)
    b = rest.astype(BF16)
    return a, b, (rest - b.astype(F32)).astype(BF16)


def call(kernel, out, cost, operands, scalars=(), slab=None, limit=24, scratch=()):
    whole = pl.BlockSpec(memory_space=pltpu.VMEM)
    specs = [whole] * len(operands)
    if slab:
        specs[0] = pl.BlockSpec(memory_space=pl.ANY)
        shape, parts = slab
        scratch = [pltpu.VMEM(shape, BF16), pltpu.SemaphoreType.DMA((parts,))]
    return pl.pallas_call(
        kernel,
        out_shape=out,
        in_specs=[pl.BlockSpec(memory_space=pltpu.SMEM)] * len(scalars) + specs,
        out_specs=jax.tree.map(lambda x: whole, out),
        scratch_shapes=scratch,
        compiler_params=pltpu.CompilerParams(vmem_limit_bytes=limit << 20),
        cost_estimate=pl.CostEstimate(flops=cost[0], bytes_accessed=cost[1], transcendentals=0),
    )(*scalars, *operands)


def in_turn(copies, work):
    for copy in copies[:2]:
        copy.start()
    for i, copy in enumerate(copies):
        copy.wait()
        if i + 2 < len(copies):
            copies[i + 2].start()
        work(i)


def flows_kernel(ptdf, *refs):
    *pieces, out = refs
    right = jnp.concatenate([piece[...] for piece in pieces], 0)
    out[...] = lax.dot_general(ptdf[...], right, NT, preferred_element_type=F32)


def dual_kernel(goes, parts, mask, sign, limit, price, out):
    flows = jnp.sum(parts[...], 0)
    scen = flows.shape[1]
    order = (lax.broadcasted_iota(jnp.int32, (scen, scen), 0) == goes[...]).astype(BF16)
    dot = lambda x: lax.dot_general(order, x, NT, preferred_element_type=F32)
    a, b, c = split3(flows)
    flows = dot(a) + dot(b) + dot(c)
    direction = (2 * sign[...] - 1).astype(F32)
    dual = (mask[...].astype(F32) * price[...] * (direction * flows - limit[...])).astype(BF16)
    for i in range(out.shape[0]):
        out[i] = dual


def cut_rows(start, ptdf, dual, slab, sems, put):
    step = slab.shape[1] // sems.shape[0]
    left = jnp.concatenate([dual[b] for b in range(dual.shape[0])], 1)

    def work(i):
        at = slice(i * step, (i + 1) * step)
        put(at, jnp.dot(left, slab[:, at], preferred_element_type=F32).T)

    in_turn(
        [
            pltpu.make_async_copy(
                ptdf.at[:, pl.ds(pl.multiple_of(start + i * step, TILE), step)],
                slab.at[:, pl.ds(i * step, step)],
                sems.at[i],
            )
            for i in range(sems.shape[0])
        ],
        work,
    )


def cuts_kernel(start, ptdf, dual, out, slab, sems):
    def put(at, rows):
        out[at, :] = rows.astype(out.dtype)

    cut_rows(start[0], ptdf, dual, slab, sems, put)


def chip_kernel(at, keep, got, to_x, to_1, to_2, to_3, stay_low, stay_high, total):
    total[...] = keep[...] + got[...].astype(F32)
    spare, x, z = at[0], at[1], at[2]
    size, half = to_x.shape[1], to_x.shape[2]

    def block(dx, dz, high):
        chip = jax.lax.rem(x + dx, 2) * 4 + jax.lax.rem(z + dz, 4)
        rows = pl.ds(pl.multiple_of(spare + chip * size, 8), size)
        return total[rows, half:] if high else total[rows, :half]

    for dz in range(4):
        to_x[dz] = block(1, dz, True).astype(BF16)
        stay_high[dz] = block(0, dz, True)
    for dx in range(2):
        stay_low[dx] = block(dx, 0, False)
        for dz, out in ((1, to_1), (2, to_2), (3, to_3)):
            out[dx] = block(dx, dz, False).astype(BF16)


def high_kernel(stay, got, to_1, to_2, to_3, mine):
    for dz, out in enumerate((mine, to_1, to_2, to_3)):
        out[...] = (stay[dz] + got[dz].astype(F32)).astype(out.dtype)


def low_kernel(stay, got_1, got_2, got_3, to_x, mine):
    for dx, out in enumerate((mine, to_x)):
        more = got_1[dx].astype(F32) + got_2[dx].astype(F32) + got_3[dx].astype(F32)
        out[...] = (stay[dx] + more).astype(out.dtype)


def pick_kernel(plan, low, got_low, high, got_1, got_2, got_3, out):
    high = high[...] + (got_1[...].astype(F32) + got_2[...].astype(F32) + got_3[...].astype(F32))
    total = jnp.concatenate([low[...] + got_low[...].astype(F32), high], 1)
    at = lax.broadcasted_iota(jnp.int32, (out.shape[0], plan.shape[1]), 0)
    pick = (at == plan[0:1, :]).astype(BF16)
    mark = (at == plan[1:2, :]).astype(BF16)
    slot = lax.broadcasted_iota(jnp.int32, (out.shape[1], plan.shape[1]), 0)
    names = jnp.where(slot == plan[2:3, :], plan[3:4, :], 0).astype(F32).astype(BF16)
    dot = lambda x: jnp.dot(pick, x, preferred_element_type=F32)
    a, b, c = split3(total)
    ids = lax.dot_general(mark, names, NT, preferred_element_type=F32)
    out[...] = dot(a) + dot(b) + dot(c) + ids


def merge_kernel(terms, out):
    rows, scen = out.shape
    count = terms.shape[0] * SLOTS
    dot = lambda x, y: jnp.dot(x, y, preferred_element_type=F32)
    iota = lambda shape, axis: lax.broadcasted_iota(jnp.int32, shape, axis)
    names = terms[:, SLOTS - 1, :TILE].astype(BF16)
    spread = (iota((count // SLOTS, count), 0) == iota((count // SLOTS, count), 1) // SLOTS).astype(
        BF16
    )
    names = lax.dot_general(names, spread, (((0,), (0,)), ((), ())), preferred_element_type=F32)
    names = jnp.where(iota((SLOTS, count), 0) == iota((SLOTS, count), 1) % SLOTS, names[:SLOTS], 0.0)
    names = jnp.sum(names, 0, keepdims=True)
    merge = (iota((rows, count), 0).astype(F32) + 1 == names).astype(BF16)
    a, b, c = split3(terms[...].reshape(count, scen))
    out[...] = dot(merge, a) + dot(merge, b) + dot(merge, c)


def local(ptdf, injections, viol_mask, viol_sign, limit, price, owner):
    line, bus = lax.axis_index("line"), lax.axis_index("bus")
    core = line % 2
    lines, buses = ptdf.shape
    rows = lines // BUSES_AT
    block = buses // LINES_AT
    half = buses // 2
    first = half // TILE * TILE
    window = buses - first
    scen = viol_mask.shape[1]
    width = scen // LINES_AT
    shape = jax.ShapeDtypeStruct
    owners = lax.dynamic_slice_in_dim(owner, (core * HALF + line // 2) * block, block, 0)
    groups, within = owners // HELD, owners % HELD
    place = ranks(groups)
    plan = jnp.stack([groups * SLOTS + place, groups * SLOTS + SLOTS - 1, place, within + 1])
    cut = lambda x: lax.dynamic_slice_in_dim(x, bus * rows, rows, 0)
    mask = cut(viol_mask).T
    sign, limit, price = (cut(x)[None, :] for x in (viol_sign, limit, price))
    goes = gathered(line, width).astype(jnp.int32)[None, :]

    pieces, (plan, mask, sign, limit, price, goes) = gather(
        injections.T, (plan, mask, sign, limit, price, goes)
    )
    work = 2 * lines * buses * scen
    step = lines // 2
    partial_flows = pl.pallas_call(
        flows_kernel,
        out_shape=shape((lines, scen), F32),
        grid=(lines // step,),
        in_specs=[pl.BlockSpec((step, buses), lambda i: (i, 0))]
        + [pl.BlockSpec(memory_space=pltpu.VMEM)] * len(pieces),
        out_specs=pl.BlockSpec((step, scen), lambda i: (i, 0)),
        compiler_params=pltpu.CompilerParams(vmem_limit_bytes=32 << 20),
        cost_estimate=pl.CostEstimate(
            flops=work, bytes_accessed=2 * lines * buses, transcendentals=0
        ),
    )(ptdf, *pieces)
    parts = lax.all_to_all(partial_flows.reshape(BUSES_AT, rows, scen), "bus", 0, 0, tiled=True)
    dual = call(
        dual_kernel,
        shape((BUSES_AT, scen, rows), BF16),
        (10 * rows * scen, 8 * lines * scen),
        (goes, parts, mask, sign, limit, price),
    )
    dual = lax.all_to_all(dual, "bus", 0, 0, tiled=True)

    def cuts(start, dtype):
        return call(
            cuts_kernel,
            shape((window, scen), dtype),
            (work // 2, lines * buses),
            (pltpu.with_memory_space_constraint(ptdf, pltpu.HBM), dual),
            (start[None],),
            slab=((lines, window), 5),
        )

    core = core.astype(jnp.int32)
    got = lax.ppermute(cuts((1 - core) * first, BF16), "line", PAIRS)
    keep = cuts(core * first, F32)
    x, z = line // 8, line // 2 % 4
    at = jnp.stack([core * (window - half), x, z]).astype(jnp.int32)
    side = scen // 2
    pile = lambda n, dtype: shape((n, block, side), dtype)
    one = lambda dtype: shape((block, side), dtype)
    small = (block * scen, 8 * block * scen)
    to_x, *to_z, stay_low, stay_high = call(
        chip_kernel,
        (pile(4, BF16), *[pile(2, BF16)] * 3, pile(2, F32), pile(4, F32)),
        (window * scen, 8 * window * scen),
        (keep, got),
        (at,),
        scratch=[pltpu.VMEM((window, scen), F32)],
    )
    go_x = lambda x: lax.ppermute(x, "line", along(1, 0, 0))
    go_z = lambda xs: [lax.ppermute(x, "line", along(0, i + 1, 0)) for i, x in enumerate(xs)]
    got_x, got_z = go_x(to_x), go_z(to_z)
    *to_z, high = call(
        high_kernel, (*[one(BF16)] * 3, one(F32)), small, (stay_high, got_x)
    )
    to_x, low = call(low_kernel, (one(BF16), one(F32)), small, (stay_low, *got_z))
    parts = low, go_x(to_x), high, *go_z(to_z)
    send = call(
        pick_kernel,
        shape((DEVICES * SLOTS, scen), F32),
        (6 * DEVICES * SLOTS * block * scen, 2 * half * scen),
        (plan, *parts),
    )
    terms = lax.all_to_all(
        send.reshape(DEVICES, SLOTS, scen), ("line", "bus"), 0, 0, tiled=True
    )
    return call(
        merge_kernel,
        shape((HELD, scen), F32),
        (6 * DEVICES * SLOTS * HELD * scen, 4 * DEVICES * SLOTS * scen),
        (terms,),
    )


def solution(mesh):
    placed = (
        P("line", "bus"),
        P("bus", "line"),
        P("line", None),
        P("line"),
        P("line"),
        P("line"),
        P("bus"),
    )
    return jax.shard_map(
        local, mesh=mesh, in_specs=placed, out_specs=P(("line", "bus"), None), check_vma=False
    )
```

```python
import jax
import jax.numpy as jnp
import numpy as np
from jax import lax
from jax.experimental import pallas as pl
from jax.experimental.pallas import tpu as pltpu
from jax.sharding import PartitionSpec as P

GENS = 10368
LINES_AT = 16
BUSES_AT = 8
DEVICES = LINES_AT * BUSES_AT
HELD = GENS // DEVICES
SLOTS = 8
TILE = 128
PAIRS = [(i, i ^ 1) for i in range(LINES_AT)]
HALF = LINES_AT // 2
BF16, F32 = jnp.bfloat16, jnp.float32
NT = (((1,), (1,)), ((), ()))


def along(dx, dz, dcore):
    pairs = []
    for x in range(2):
        for z in range(4):
            for core in range(2):
                to = ((x + dx) % 2, (z + dz) % 4, (core + dcore) % 2)
                pairs.append((x * 8 + z * 2 + core, to[0] * 8 + to[1] * 2 + to[2]))
    return pairs


ORDER = [
    [(0, 0, 0), (0, 0, 1), (1, 0, 0), (1, 0, 1), (0, 3, 1), (0, 1, 1)],
    [(0, 3, 0), (1, 3, 0), (0, 1, 0), (1, 1, 0), (1, 3, 1), (1, 1, 1)],
    [(0, 2, 1), (1, 2, 1), (0, 2, 0), (1, 2, 0)],
]


def gather(block, ready):
    move = lambda x, *to: lax.ppermute(x, "line", along(*to))
    stack = lambda *x: jnp.concatenate(x, 0)
    half = block.shape[0] // 2
    low, high = block[:half], block[half:]
    low_x = move(low, 1, 0, 0)
    high, low_x = lax.optimization_barrier((high, low_x))
    high_x = move(high, 1, 0, 0)
    high_1, high_3 = move(high, 0, 1, 0), move(high, 0, 3, 0)
    high_2 = move(high_1, 0, 1, 0)
    pair = stack(low, low_x)
    pair_1, pair_3 = move(pair, 0, 1, 0), move(pair, 0, 3, 0)
    high_z = stack(high_1, high_3)
    high_zx = move(high_z, 1, 0, 0)
    high_2x = move(high_2, 1, 0, 0)
    pair_1, pair_3, ready = lax.optimization_barrier((pair_1, pair_3, ready))
    low_2, beside_2 = move(pair_1[:half], 0, 1, 0), move(pair_3[half:], 0, 3, 0)
    pieces = [
        stack(block, low_x, high_x, high_z),
        stack(pair_1, pair_3, high_zx),
        stack(high_2, high_2x, low_2, beside_2),
    ]
    return pieces + [move(piece, 0, 0, 1) for piece in pieces], ready


def gathered(line, width):
    spots = np.array([(*at, core) for core in (0, 1) for at in sum(ORDER, [])])
    dx, dz, half, core = (np.repeat(spots[:, i], width // 2) for i in range(4))
    at = np.arange(dx.shape[0]) % (width // 2) + half * (width // 2)
    x, z, mine = line // 8, line // 2 % 4, line % 2
    device = (x + dx) % 2 * 8 + (z + dz) % 4 * 2 + (mine + core) % 2
    return device * width + at


def ranks(groups):
    count = groups.shape[-1]
    same = groups[..., :, None] == groups[..., None, :]
    earlier = lax.broadcasted_iota(jnp.int32, (count, count), 0) > lax.broadcasted_iota(
        jnp.int32, (count, count), 1
    )
    return jnp.sum((same & earlier).astype(jnp.int32), axis=-1)


def split3(x):
    a = x.astype(BF16)
    rest = x - a.astype(F32)
    b = rest.astype(BF16)
    return a, b, (rest - b.astype(F32)).astype(BF16)


def call(kernel, out, cost, operands, scalars=(), slab=None, limit=24, scratch=()):
    whole = pl.BlockSpec(memory_space=pltpu.VMEM)
    specs = [whole] * len(operands)
    if slab:
        specs[0] = pl.BlockSpec(memory_space=pl.ANY)
        shape, parts = slab
        scratch = [pltpu.VMEM(shape, BF16), pltpu.SemaphoreType.DMA((parts,))]
    return pl.pallas_call(
        kernel,
        out_shape=out,
        in_specs=[pl.BlockSpec(memory_space=pltpu.SMEM)] * len(scalars) + specs,
        out_specs=jax.tree.map(lambda x: whole, out),
        scratch_shapes=scratch,
        compiler_params=pltpu.CompilerParams(vmem_limit_bytes=limit << 20),
        cost_estimate=pl.CostEstimate(flops=cost[0], bytes_accessed=cost[1], transcendentals=0),
    )(*scalars, *operands)


def in_turn(copies, work):
    for copy in copies[:2]:
        copy.start()
    for i, copy in enumerate(copies):
        copy.wait()
        if i + 2 < len(copies):
            copies[i + 2].start()
        work(i)


def flows_kernel(ptdf, *refs):
    *pieces, out = refs
    right = jnp.concatenate([piece[...] for piece in pieces], 0)
    out[...] = lax.dot_general(ptdf[...], right, NT, preferred_element_type=F32)


def dual_kernel(goes, parts, mask, sign, limit, price, out):
    flows = jnp.sum(parts[...], 0)
    scen = flows.shape[1]
    order = (lax.broadcasted_iota(jnp.int32, (scen, scen), 0) == goes[...]).astype(BF16)
    dot = lambda x: lax.dot_general(order, x, NT, preferred_element_type=F32)
    a, b, c = split3(flows)
    flows = dot(a) + dot(b) + dot(c)
    direction = (2 * sign[...] - 1).astype(F32)
    dual = (mask[...].astype(F32) * price[...] * (direction * flows - limit[...])).astype(BF16)
    for i in range(out.shape[0]):
        out[i] = dual


def cut_rows(start, ptdf, dual, slab, sems, put):
    step = slab.shape[1] // sems.shape[0]
    left = jnp.concatenate([dual[b] for b in range(dual.shape[0])], 1)

    def work(i):
        at = slice(i * step, (i + 1) * step)
        put(at, jnp.dot(left, slab[:, at], preferred_element_type=F32).T)

    in_turn(
        [
            pltpu.make_async_copy(
                ptdf.at[:, pl.ds(pl.multiple_of(start + i * step, TILE), step)],
                slab.at[:, pl.ds(i * step, step)],
                sems.at[i],
            )
            for i in range(sems.shape[0])
        ],
        work,
    )


def cuts_kernel(start, ptdf, dual, out, slab, sems):
    def put(at, rows):
        out[at, :] = rows.astype(out.dtype)

    cut_rows(start[0], ptdf, dual, slab, sems, put)


def chip_kernel(at, keep, got, to_x, to_1, to_2, to_3, stay_low, stay_high, total):
    total[...] = keep[...] + got[...].astype(F32)
    spare, x, z = at[0], at[1], at[2]
    size, half = to_x.shape[1], to_x.shape[2]

    def block(dx, dz, high):
        chip = jax.lax.rem(x + dx, 2) * 4 + jax.lax.rem(z + dz, 4)
        rows = pl.ds(pl.multiple_of(spare + chip * size, 8), size)
        return total[rows, half:] if high else total[rows, :half]

    for dz in range(4):
        to_x[dz] = block(1, dz, True).astype(BF16)
        stay_high[dz] = block(0, dz, True)
    for dx in range(2):
        stay_low[dx] = block(dx, 0, False)
        for dz, out in ((1, to_1), (2, to_2), (3, to_3)):
            out[dx] = block(dx, dz, False).astype(BF16)


def high_kernel(stay, got, to_1, to_2, to_3, mine):
    for dz, out in enumerate((mine, to_1, to_2, to_3)):
        out[...] = (stay[dz] + got[dz].astype(F32)).astype(out.dtype)


def low_kernel(stay, got_1, got_2, got_3, to_x, mine):
    for dx, out in enumerate((mine, to_x)):
        more = got_1[dx].astype(F32) + got_2[dx].astype(F32) + got_3[dx].astype(F32)
        out[...] = (stay[dx] + more).astype(out.dtype)


def pick_kernel(plan, low, got_low, high, got_1, got_2, got_3, out):
    high = high[...] + (got_1[...].astype(F32) + got_2[...].astype(F32) + got_3[...].astype(F32))
    total = jnp.concatenate([low[...] + got_low[...].astype(F32), high], 1)
    at = lax.broadcasted_iota(jnp.int32, (out.shape[0], plan.shape[1]), 0)
    pick = (at == plan[0:1, :]).astype(BF16)
    mark = (at == plan[1:2, :]).astype(BF16)
    slot = lax.broadcasted_iota(jnp.int32, (out.shape[1], plan.shape[1]), 0)
    names = jnp.where(slot == plan[2:3, :], plan[3:4, :], 0).astype(F32).astype(BF16)
    dot = lambda x: jnp.dot(pick, x, preferred_element_type=F32)
    a, b, c = split3(total)
    ids = lax.dot_general(mark, names, NT, preferred_element_type=F32)
    out[...] = dot(a) + dot(b) + dot(c) + ids


def merge_kernel(terms, out):
    rows, scen = out.shape
    count = terms.shape[0] * SLOTS
    dot = lambda x, y: jnp.dot(x, y, preferred_element_type=F32)
    iota = lambda shape, axis: lax.broadcasted_iota(jnp.int32, shape, axis)
    names = terms[:, SLOTS - 1, :TILE].astype(BF16)
    spread = (iota((count // SLOTS, count), 0) == iota((count // SLOTS, count), 1) // SLOTS).astype(
        BF16
    )
    names = lax.dot_general(names, spread, (((0,), (0,)), ((), ())), preferred_element_type=F32)
    names = jnp.where(iota((SLOTS, count), 0) == iota((SLOTS, count), 1) % SLOTS, names[:SLOTS], 0.0)
    names = jnp.sum(names, 0, keepdims=True)
    merge = (iota((rows, count), 0).astype(F32) + 1 == names).astype(BF16)
    a, b, c = split3(terms[...].reshape(count, scen))
    out[...] = dot(merge, a) + dot(merge, b) + dot(merge, c)


def local(ptdf, injections, viol_mask, viol_sign, limit, price, owner):
    line, bus = lax.axis_index("line"), lax.axis_index("bus")
    core = line % 2
    lines, buses = ptdf.shape
    rows = lines // BUSES_AT
    block = buses // LINES_AT
    half = buses // 2
    first = half // TILE * TILE
    window = buses - first
    scen = viol_mask.shape[1]
    width = scen // LINES_AT
    shape = jax.ShapeDtypeStruct
    owners = lax.dynamic_slice_in_dim(owner, (core * HALF + line // 2) * block, block, 0)
    groups, within = owners // HELD, owners % HELD
    place = ranks(groups)
    plan = jnp.stack([groups * SLOTS + place, groups * SLOTS + SLOTS - 1, place, within + 1])
    cut = lambda x: lax.dynamic_slice_in_dim(x, bus * rows, rows, 0)
    mask = cut(viol_mask).T
    sign, limit, price = (cut(x)[None, :] for x in (viol_sign, limit, price))
    goes = gathered(line, width).astype(jnp.int32)[None, :]

    pieces, (plan, mask, sign, limit, price, goes) = gather(
        injections.T, (plan, mask, sign, limit, price, goes)
    )
    work = 2 * lines * buses * scen
    step = lines // 2
    partial_flows = pl.pallas_call(
        flows_kernel,
        out_shape=shape((lines, scen), F32),
        grid=(lines // step,),
        in_specs=[pl.BlockSpec((step, buses), lambda i: (i, 0))]
        + [pl.BlockSpec(memory_space=pltpu.VMEM)] * len(pieces),
        out_specs=pl.BlockSpec((step, scen), lambda i: (i, 0)),
        compiler_params=pltpu.CompilerParams(vmem_limit_bytes=32 << 20),
        cost_estimate=pl.CostEstimate(
            flops=work, bytes_accessed=2 * lines * buses, transcendentals=0
        ),
    )(ptdf, *pieces)
    parts = lax.all_to_all(partial_flows.reshape(BUSES_AT, rows, scen), "bus", 0, 0, tiled=True)
    dual = call(
        dual_kernel,
        shape((BUSES_AT, scen, rows), BF16),
        (10 * rows * scen, 8 * lines * scen),
        (goes, parts, mask, sign, limit, price),
    )
    dual = lax.all_to_all(dual, "bus", 0, 0, tiled=True)

    def cuts(start, dtype):
        return call(
            cuts_kernel,
            shape((window, scen), dtype),
            (work // 2, lines * buses),
            (pltpu.with_memory_space_constraint(ptdf, pltpu.HBM), dual),
            (start[None],),
            slab=((lines, window), 5),
        )

    core = core.astype(jnp.int32)
    got = lax.ppermute(cuts((1 - core) * first, BF16), "line", PAIRS)
    keep = cuts(core * first, F32)
    x, z = line // 8, line // 2 % 4
    at = jnp.stack([core * (window - half), x, z]).astype(jnp.int32)
    side = scen // 2
    pile = lambda n, dtype: shape((n, block, side), dtype)
    one = lambda dtype: shape((block, side), dtype)
    small = (block * scen, 8 * block * scen)
    to_x, *to_z, stay_low, stay_high = call(
        chip_kernel,
        (pile(4, BF16), *[pile(2, BF16)] * 3, pile(2, F32), pile(4, F32)),
        (window * scen, 8 * window * scen),
        (keep, got),
        (at,),
        scratch=[pltpu.VMEM((window, scen), F32)],
    )
    go_x = lambda x: lax.ppermute(x, "line", along(1, 0, 0))
    go_z = lambda xs: [lax.ppermute(x, "line", along(0, i + 1, 0)) for i, x in enumerate(xs)]
    got_x, got_z = go_x(to_x), go_z(to_z)
    *to_z, high = call(
        high_kernel, (*[one(BF16)] * 3, one(F32)), small, (stay_high, got_x)
    )
    to_x, low = call(low_kernel, (one(BF16), one(F32)), small, (stay_low, *got_z))
    parts = low, go_x(to_x), high, *go_z(to_z)
    send = call(
        pick_kernel,
        shape((DEVICES * SLOTS, scen), F32),
        (6 * DEVICES * SLOTS * block * scen, 2 * half * scen),
        (plan, *parts),
    )
    terms = lax.all_to_all(
        send.reshape(DEVICES, SLOTS, scen), ("line", "bus"), 0, 0, tiled=True
    )
    return call(
        merge_kernel,
        shape((HELD, scen), F32),
        (6 * DEVICES * SLOTS * HELD * scen, 4 * DEVICES * SLOTS * scen),
        (terms,),
    )


def solution(mesh):
    placed = (
        P("line", "bus"),
        P("bus", "line"),
        P("line", None),
        P("line"),
        P("line"),
        P("line"),
        P("bus"),
    )
    return jax.shard_map(
        local, mesh=mesh, in_specs=placed, out_specs=P(("line", "bus"), None), check_vma=False
    )
```

```python
import jax
import jax.numpy as jnp
import numpy as np
from jax import lax
from jax.experimental import pallas as pl
from jax.experimental.pallas import tpu as pltpu
from jax.sharding import PartitionSpec as P

GENS = 10368
LINES_AT = 16
BUSES_AT = 8
DEVICES = LINES_AT * BUSES_AT
HELD = GENS // DEVICES
SLOTS = 8
TILE = 128
PAIRS = [(i, i ^ 1) for i in range(LINES_AT)]
HALF = LINES_AT // 2
BF16, F32 = jnp.bfloat16, jnp.float32
NT = (((1,), (1,)), ((), ()))


def along(dx, dz, dcore):
    pairs = []
    for x in range(2):
        for z in range(4):
            for core in range(2):
                to = ((x + dx) % 2, (z + dz) % 4, (core + dcore) % 2)
                pairs.append((x * 8 + z * 2 + core, to[0] * 8 + to[1] * 2 + to[2]))
    return pairs


ORDER = [
    [(0, 0, 0), (0, 0, 1), (1, 0, 0), (1, 0, 1), (0, 3, 1), (0, 1, 1)],
    [(0, 3, 0), (1, 3, 0), (0, 1, 0), (1, 1, 0), (1, 3, 1), (1, 1, 1)],
    [(0, 2, 1), (1, 2, 1), (0, 2, 0), (1, 2, 0)],
]


def gather(block, ready):
    move = lambda x, *to: lax.ppermute(x, "line", along(*to))
    stack = lambda *x: jnp.concatenate(x, 0)
    half = block.shape[0] // 2
    low, high = block[:half], block[half:]
    low_x = move(low, 1, 0, 0)
    high, low_x = lax.optimization_barrier((high, low_x))
    high_x = move(high, 1, 0, 0)
    pair = stack(low, low_x)
    high, pair = lax.optimization_barrier((high, pair))
    pair_1, pair_3 = move(pair, 0, 1, 0), move(pair, 0, 3, 0)
    high_1, high_3 = move(high, 0, 1, 0), move(high, 0, 3, 0)
    high_2 = move(high_1, 0, 1, 0)
    high_z = stack(high_1, high_3)
    high_zx = move(high_z, 1, 0, 0)
    high_2x = move(high_2, 1, 0, 0)
    pair_1, pair_3, ready = lax.optimization_barrier((pair_1, pair_3, ready))
    low_2, beside_2 = move(pair_1[:half], 0, 1, 0), move(pair_3[half:], 0, 3, 0)
    pieces = [
        stack(block, low_x, high_x, high_z),
        stack(pair_1, pair_3, high_zx),
        stack(high_2, high_2x, low_2, beside_2),
    ]
    return pieces + [move(piece, 0, 0, 1) for piece in pieces], ready


def gathered(line, width):
    spots = np.array([(*at, core) for core in (0, 1) for at in sum(ORDER, [])])
    dx, dz, half, core = (np.repeat(spots[:, i], width // 2) for i in range(4))
    at = np.arange(dx.shape[0]) % (width // 2) + half * (width // 2)
    x, z, mine = line // 8, line // 2 % 4, line % 2
    device = (x + dx) % 2 * 8 + (z + dz) % 4 * 2 + (mine + core) % 2
    return device * width + at


def ranks(groups):
    count = groups.shape[-1]
    same = groups[..., :, None] == groups[..., None, :]
    earlier = lax.broadcasted_iota(jnp.int32, (count, count), 0) > lax.broadcasted_iota(
        jnp.int32, (count, count), 1
    )
    return jnp.sum((same & earlier).astype(jnp.int32), axis=-1)


def split3(x):
    a = x.astype(BF16)
    rest = x - a.astype(F32)
    b = rest.astype(BF16)
    return a, b, (rest - b.astype(F32)).astype(BF16)


def call(kernel, out, cost, operands, scalars=(), slab=None, limit=24, scratch=()):
    whole = pl.BlockSpec(memory_space=pltpu.VMEM)
    specs = [whole] * len(operands)
    if slab:
        specs[0] = pl.BlockSpec(memory_space=pl.ANY)
        shape, parts = slab
        scratch = [pltpu.VMEM(shape, BF16), pltpu.SemaphoreType.DMA((parts,))]
    return pl.pallas_call(
        kernel,
        out_shape=out,
        in_specs=[pl.BlockSpec(memory_space=pltpu.SMEM)] * len(scalars) + specs,
        out_specs=jax.tree.map(lambda x: whole, out),
        scratch_shapes=scratch,
        compiler_params=pltpu.CompilerParams(vmem_limit_bytes=limit << 20),
        cost_estimate=pl.CostEstimate(flops=cost[0], bytes_accessed=cost[1], transcendentals=0),
    )(*scalars, *operands)


def in_turn(copies, work):
    for copy in copies[:2]:
        copy.start()
    for i, copy in enumerate(copies):
        copy.wait()
        if i + 2 < len(copies):
            copies[i + 2].start()
        work(i)


def flows_kernel(ptdf, *refs):
    *pieces, out = refs
    right = jnp.concatenate([piece[...] for piece in pieces], 0)
    out[...] = lax.dot_general(ptdf[...], right, NT, preferred_element_type=F32)


def dual_kernel(goes, parts, mask, sign, limit, price, out):
    flows = jnp.sum(parts[...], 0)
    scen = flows.shape[1]
    order = (lax.broadcasted_iota(jnp.int32, (scen, scen), 0) == goes[...]).astype(BF16)
    dot = lambda x: lax.dot_general(order, x, NT, preferred_element_type=F32)
    a, b, c = split3(flows)
    flows = dot(a) + dot(b) + dot(c)
    direction = (2 * sign[...] - 1).astype(F32)
    dual = (mask[...].astype(F32) * price[...] * (direction * flows - limit[...])).astype(BF16)
    for i in range(out.shape[0]):
        out[i] = dual


def cut_rows(start, ptdf, dual, slab, sems, put):
    step = slab.shape[1] // sems.shape[0]
    left = jnp.concatenate([dual[b] for b in range(dual.shape[0])], 1)

    def work(i):
        at = slice(i * step, (i + 1) * step)
        put(at, jnp.dot(left, slab[:, at], preferred_element_type=F32).T)

    in_turn(
        [
            pltpu.make_async_copy(
                ptdf.at[:, pl.ds(pl.multiple_of(start + i * step, TILE), step)],
                slab.at[:, pl.ds(i * step, step)],
                sems.at[i],
            )
            for i in range(sems.shape[0])
        ],
        work,
    )


def cuts_kernel(start, ptdf, dual, out, slab, sems):
    def put(at, rows):
        out[at, :] = rows.astype(out.dtype)

    cut_rows(start[0], ptdf, dual, slab, sems, put)


def chip_kernel(at, keep, got, to_x, to_1, to_2, to_3, stay_low, stay_high, total):
    total[...] = keep[...] + got[...].astype(F32)
    spare, x, z = at[0], at[1], at[2]
    size, half = to_x.shape[1], to_x.shape[2]

    def block(dx, dz, high):
        chip = jax.lax.rem(x + dx, 2) * 4 + jax.lax.rem(z + dz, 4)
        rows = pl.ds(pl.multiple_of(spare + chip * size, 8), size)
        return total[rows, half:] if high else total[rows, :half]

    for dz in range(4):
        to_x[dz] = block(1, dz, True).astype(BF16)
        stay_high[dz] = block(0, dz, True)
    for dx in range(2):
        stay_low[dx] = block(dx, 0, False)
        for dz, out in ((1, to_1), (2, to_2), (3, to_3)):
            out[dx] = block(dx, dz, False).astype(BF16)


def high_kernel(stay, got, to_1, to_2, to_3, mine):
    for dz, out in enumerate((mine, to_1, to_2, to_3)):
        out[...] = (stay[dz] + got[dz].astype(F32)).astype(out.dtype)


def low_kernel(stay, got_1, got_2, got_3, to_x, mine):
    for dx, out in enumerate((mine, to_x)):
        more = got_1[dx].astype(F32) + got_2[dx].astype(F32) + got_3[dx].astype(F32)
        out[...] = (stay[dx] + more).astype(out.dtype)


def pick_kernel(plan, low, got_low, high, got_1, got_2, got_3, out):
    high = high[...] + (got_1[...].astype(F32) + got_2[...].astype(F32) + got_3[...].astype(F32))
    total = jnp.concatenate([low[...] + got_low[...].astype(F32), high], 1)
    at = lax.broadcasted_iota(jnp.int32, (out.shape[0], plan.shape[1]), 0)
    pick = (at == plan[0:1, :]).astype(BF16)
    mark = (at == plan[1:2, :]).astype(BF16)
    slot = lax.broadcasted_iota(jnp.int32, (out.shape[1], plan.shape[1]), 0)
    names = jnp.where(slot == plan[2:3, :], plan[3:4, :], 0).astype(F32).astype(BF16)
    dot = lambda x: jnp.dot(pick, x, preferred_element_type=F32)
    a, b, c = split3(total)
    ids = lax.dot_general(mark, names, NT, preferred_element_type=F32)
    out[...] = dot(a) + dot(b) + dot(c) + ids


def merge_kernel(terms, out):
    rows, scen = out.shape
    count = terms.shape[0] * SLOTS
    dot = lambda x, y: jnp.dot(x, y, preferred_element_type=F32)
    iota = lambda shape, axis: lax.broadcasted_iota(jnp.int32, shape, axis)
    names = terms[:, SLOTS - 1, :TILE].astype(BF16)
    spread = (iota((count // SLOTS, count), 0) == iota((count // SLOTS, count), 1) // SLOTS).astype(
        BF16
    )
    names = lax.dot_general(names, spread, (((0,), (0,)), ((), ())), preferred_element_type=F32)
    names = jnp.where(iota((SLOTS, count), 0) == iota((SLOTS, count), 1) % SLOTS, names[:SLOTS], 0.0)
    names = jnp.sum(names, 0, keepdims=True)
    merge = (iota((rows, count), 0).astype(F32) + 1 == names).astype(BF16)
    a, b, c = split3(terms[...].reshape(count, scen))
    out[...] = dot(merge, a) + dot(merge, b) + dot(merge, c)


def local(ptdf, injections, viol_mask, viol_sign, limit, price, owner):
    line, bus = lax.axis_index("line"), lax.axis_index("bus")
    core = line % 2
    lines, buses = ptdf.shape
    rows = lines // BUSES_AT
    block = buses // LINES_AT
    half = buses // 2
    first = half // TILE * TILE
    window = buses - first
    scen = viol_mask.shape[1]
    width = scen // LINES_AT
    shape = jax.ShapeDtypeStruct
    owners = lax.dynamic_slice_in_dim(owner, (core * HALF + line // 2) * block, block, 0)
    groups, within = owners // HELD, owners % HELD
    place = ranks(groups)
    plan = jnp.stack([groups * SLOTS + place, groups * SLOTS + SLOTS - 1, place, within + 1])
    cut = lambda x: lax.dynamic_slice_in_dim(x, bus * rows, rows, 0)
    mask = cut(viol_mask).T
    sign, limit, price = (cut(x)[None, :] for x in (viol_sign, limit, price))
    goes = gathered(line, width).astype(jnp.int32)[None, :]

    pieces, (plan, mask, sign, limit, price, goes) = gather(
        injections.T, (plan, mask, sign, limit, price, goes)
    )
    work = 2 * lines * buses * scen
    step = lines // 2
    partial_flows = pl.pallas_call(
        flows_kernel,
        out_shape=shape((lines, scen), F32),
        grid=(lines // step,),
        in_specs=[pl.BlockSpec((step, buses), lambda i: (i, 0))]
        + [pl.BlockSpec(memory_space=pltpu.VMEM)] * len(pieces),
        out_specs=pl.BlockSpec((step, scen), lambda i: (i, 0)),
        compiler_params=pltpu.CompilerParams(vmem_limit_bytes=32 << 20),
        cost_estimate=pl.CostEstimate(
            flops=work, bytes_accessed=2 * lines * buses, transcendentals=0
        ),
    )(ptdf, *pieces)
    parts = lax.all_to_all(partial_flows.reshape(BUSES_AT, rows, scen), "bus", 0, 0, tiled=True)
    dual = call(
        dual_kernel,
        shape((BUSES_AT, scen, rows), BF16),
        (10 * rows * scen, 8 * lines * scen),
        (goes, parts, mask, sign, limit, price),
    )
    dual = lax.all_to_all(dual, "bus", 0, 0, tiled=True)

    def cuts(start, dtype):
        return call(
            cuts_kernel,
            shape((window, scen), dtype),
            (work // 2, lines * buses),
            (pltpu.with_memory_space_constraint(ptdf, pltpu.HBM), dual),
            (start[None],),
            slab=((lines, window), 5),
        )

    core = core.astype(jnp.int32)
    got = lax.ppermute(cuts((1 - core) * first, BF16), "line", PAIRS)
    keep = cuts(core * first, F32)
    x, z = line // 8, line // 2 % 4
    at = jnp.stack([core * (window - half), x, z]).astype(jnp.int32)
    side = scen // 2
    pile = lambda n, dtype: shape((n, block, side), dtype)
    one = lambda dtype: shape((block, side), dtype)
    small = (block * scen, 8 * block * scen)
    to_x, *to_z, stay_low, stay_high = call(
        chip_kernel,
        (pile(4, BF16), *[pile(2, BF16)] * 3, pile(2, F32), pile(4, F32)),
        (window * scen, 8 * window * scen),
        (keep, got),
        (at,),
        scratch=[pltpu.VMEM((window, scen), F32)],
    )
    go_x = lambda x: lax.ppermute(x, "line", along(1, 0, 0))
    go_z = lambda xs: [lax.ppermute(x, "line", along(0, i + 1, 0)) for i, x in enumerate(xs)]
    got_x, got_z = go_x(to_x), go_z(to_z)
    *to_z, high = call(
        high_kernel, (*[one(BF16)] * 3, one(F32)), small, (stay_high, got_x)
    )
    got_z, to_z = lax.optimization_barrier((got_z, to_z))
    to_x, low = call(low_kernel, (one(BF16), one(F32)), small, (stay_low, *got_z))
    parts = low, go_x(to_x), high, *go_z(to_z)
    send = call(
        pick_kernel,
        shape((DEVICES * SLOTS, scen), F32),
        (6 * DEVICES * SLOTS * block * scen, 2 * half * scen),
        (plan, *parts),
    )
    terms = lax.all_to_all(
        send.reshape(DEVICES, SLOTS, scen), ("line", "bus"), 0, 0, tiled=True
    )
    return call(
        merge_kernel,
        shape((HELD, scen), F32),
        (6 * DEVICES * SLOTS * HELD * scen, 4 * DEVICES * SLOTS * scen),
        (terms,),
    )


def solution(mesh):
    placed = (
        P("line", "bus"),
        P("bus", "line"),
        P("line", None),
        P("line"),
        P("line"),
        P("line"),
        P("bus"),
    )
    return jax.shard_map(
        local, mesh=mesh, in_specs=placed, out_specs=P(("line", "bus"), None), check_vma=False
    )
```
